32 devices in a mesh: gx: 4 (over z), gy: 4 (over y, x), gz: 2 (over core).
Axes of the slice: x: 2, y: 2, z: 4, core: 2. Of those that a mesh axis runs over, the one named last changes fastest.
Arguments:
- adj_e: float32 [2, 3, 32, 64, 512], P(None, None, 'gy', 'gz', 'gx'), may hold values from -6 to 6
- adj_h: float32 [2, 3, 32, 64, 512], P(None, None, 'gy', 'gz', 'gx'), may hold values from -6 to 6
- fwd_e: bfloat16 [2, 2, 3, 32, 64, 512], P(None, None, None, 'gy', 'gz', 'gx'), may hold values from -6 to 6
- material: int32 [32, 64, 512], P('gy', 'gz', 'gx'), may hold values from 0 to 3
- eps_table: float32 [4], replicated, may hold values from 0.6 to 1
Outputs:
- new_e: float32 [2, 3, 32, 64, 512], P(None, None, 'gy', 'gz', 'gx')
- new_h: float32 [2, 3, 32, 64, 512], P(None, None, 'gy', 'gz', 'gx')
- grad_eps: float32 [32, 64, 512], P('gy', 'gz', 'gx')
The draws below stay inside these ranges and needn't reach their ends.
Inputs may be any that keep to these rules, and one draw needn't show every extreme that they name: `material`: a valid index into eps_table.
All inputs are finite; a program needn't handle non-finite values.
Results may differ from the reference program's by a relative error of at most 0.0003.
Values sent between devices are 32-bit elements; how exact they have to be, the bound alone decides.
A program may use at most 128 MiB of HBM per device.

```python
import math
import jax
import jax.numpy as jnp
from jax import lax

STEPS = 2
MATS = 4
NX = 512
NY = 32
NZ = 64


def touch_ends(entries, stream_key, smallest, largest):
    place = [jax.random.randint(jax.random.fold_in(stream_key, axis), (), 0, length) for axis, length in enumerate(entries.shape)]
    widest = entries.shape.index(max(entries.shape))
    beside = place[:widest] + [(place[widest] + 1) % entries.shape[widest]] + place[widest + 1:]
    return entries.at[tuple(place)].set(smallest).at[tuple(beside)].set(largest)


def level_of(rng, shape, shards, smallest, high):
    def one(axis_at, parts):
        heights = jax.random.uniform(jax.random.fold_in(jax.random.fold_in(rng, 6), axis_at), (parts,), jnp.float32, smallest / len(shards), high / len(shards))
        return jnp.repeat(jnp.exp(heights), shape[axis_at] // parts).reshape((-1,) + (1,) * (len(shape) - axis_at - 1))

    factor_of = one(*shards[0])
    for cut in shards[1:]:
        factor_of = factor_of * one(*cut)
    return factor_of


def centred(key, shape, width, bound, cuts=(), held_as=jnp.bfloat16):
    array = width * jax.random.normal(key, shape, jnp.float32)
    if cuts:
        array = array * level_of(key, shape, cuts, -0.22, 0.18)
    return jnp.clip(array, -bound, bound).astype(held_as)


def setup_inputs(seed: int = 0) -> dict:
    splits = jax.random.split(jax.random.key(seed), 6)
    adj_e = centred(splits[0], (2, 3, NY, NZ, NX), 1.0, 6.0, ((2, 4), (3, 2), (4, 4)), jnp.float32)
    adj_h = centred(splits[1], (2, 3, NY, NZ, NX), 1.0, 6.0, ((2, 4), (3, 2), (4, 4)), jnp.float32)
    fwd_e = centred(splits[2], (STEPS, 2, 3, NY, NZ, NX), 1.0, 6.0, ((3, 4), (4, 2), (5, 4)))
    material = touch_ends(jax.random.randint(splits[3], (NY, NZ, NX), 0, MATS), jax.random.fold_in(splits[3], 1), 0, MATS - 1).astype(jnp.int32)
    eps_table = jnp.clip(jax.random.uniform(splits[4], (MATS,), jnp.float32, 0.6, 1.0), 0.6, 1.0)
    return dict(adj_e=adj_e, adj_h=adj_h, fwd_e=fwd_e, material=material, eps_table=eps_table)


time_step = 0.4
phase_x = 1.3
phase_y = 0.7


def rotate_pair(pair, cosine, sine):
    return jnp.stack([pair[0] * cosine - pair[1] * sine, pair[0] * sine + pair[1] * cosine])


def behind(field, axis, phase, periodic):
    rolled = jnp.roll(field, 1, axis)
    places = lax.broadcasted_iota(jnp.int32, field.shape, axis)
    first = places == 0
    if periodic:
        return jnp.where(first, rotate_pair(rolled, math.cos(phase), -math.sin(phase)), rolled)
    return jnp.where(first, jnp.float32(0.0), rolled)


def ahead(field, axis, phase, periodic):
    rolled = jnp.roll(field, -1, axis)
    places = lax.broadcasted_iota(jnp.int32, field.shape, axis)
    final = places == field.shape[axis] - 1
    if periodic:
        return jnp.where(final, rotate_pair(rolled, math.cos(phase), math.sin(phase)), rolled)
    return jnp.where(final, jnp.float32(0.0), rolled)


def back_y(field):
    return field - behind(field, 1, phase_y, True)


def back_z(field):
    return field - behind(field, 2, 0.0, False)


def back_x(field):
    return field - behind(field, 3, phase_x, True)


def fore_y(field):
    return ahead(field, 1, phase_y, True) - field


def fore_z(field):
    return ahead(field, 2, 0.0, False) - field


def fore_x(field):
    return ahead(field, 3, phase_x, True) - field


def reference(adj_e, adj_h, fwd_e, material, eps_table):
    inverse_eps = jnp.take(1.0 / eps_table, material)
    e_field = adj_e
    h_field = adj_h
    grad_eps = jnp.zeros(material.shape, jnp.float32)
    for section in range(STEPS):
        h_xcomp, h_ycomp, h_zcomp = h_field[:, 0], h_field[:, 1], h_field[:, 2]
        curl_x = back_y(h_zcomp) - back_z(h_ycomp)
        curl_y = back_z(h_xcomp) - back_x(h_zcomp)
        curl_z = back_x(h_ycomp) - back_y(h_xcomp)
        e_field = e_field - time_step * inverse_eps * jnp.stack([curl_x, curl_y, curl_z], 1)
        grad_eps = grad_eps + inverse_eps * jnp.sum(e_field * fwd_e[section].astype(jnp.float32), axis=(0, 1))
        e_xcomp, e_ycomp, e_zcomp = e_field[:, 0], e_field[:, 1], e_field[:, 2]
        rise_x = fore_y(e_zcomp) - fore_z(e_ycomp)
        rise_y = fore_z(e_xcomp) - fore_x(e_zcomp)
        rise_z = fore_x(e_ycomp) - fore_y(e_xcomp)
        h_field = h_field + time_step * jnp.stack([rise_x, rise_y, rise_z], 1)
    return e_field, h_field, grad_eps
```

```python
import functools
import math

import jax
import jax.numpy as jnp
from jax import lax
from jax.experimental import pallas as pl
from jax.experimental.pallas import tpu as pltpu
from jax.sharding import PartitionSpec as P

time_step = 0.4
phase_x = 1.3
phase_y = 0.7
MESH = pl.DeviceIdType.MESH


def kernel(counts, eps, e_in, h_in, fwd_in, mat_in, e, h, g,
           fwd, mat, inv, xs, xr, yr, zs, zr, load_sem, send_sem, recv_sem):
    steps = fwd.shape[0]
    ny, nz, nx = mat.shape
    place = {a: lax.axis_index(a) for a in counts}
    after = {a: lax.rem(place[a] + 1, counts[a]) for a in counts}
    before = {a: lax.rem(place[a] + counts[a] - 1, counts[a]) for a in counts}

    loads = [
        pltpu.make_async_copy(h_in, h, load_sem.at[0]),
        pltpu.make_async_copy(e_in, e, load_sem.at[1]),
        pltpu.make_async_copy(mat_in, mat, load_sem.at[2]),
        pltpu.make_async_copy(fwd_in, fwd, load_sem.at[3]),
    ]
    for load in loads:
        load.start()

    barrier = pltpu.get_barrier_semaphore()
    greeted = 0
    for a in counts:
        pl.semaphore_signal(barrier, inc=1, device_id={a: after[a]}, device_id_type=MESH)
        greeted += 1
        if counts[a] > 2:
            pl.semaphore_signal(barrier, inc=1, device_id={a: before[a]}, device_id_type=MESH)
            greeted += 1
    pl.semaphore_wait(barrier, greeted)

    def remote(r, which, src, dst, axis):
        to = after[axis] if r % 2 == 0 else before[axis]
        return pltpu.make_async_remote_copy(
            src_ref=src, dst_ref=dst, send_sem=send_sem.at[r, which],
            recv_sem=recv_sem.at[r, which], device_id={axis: to}, device_id_type=MESH)

    def copies(r, field):
        edge = ny - 1 if r % 2 == 0 else 0
        return dict(
            x=remote(r, 0, xs.at[r], xr.at[r], "gx"),
            y0=remote(r, 1, field.at[:, 0, edge], yr.at[r, 0], "gy"),
            y1=remote(r, 2, field.at[:, 2, edge], yr.at[r, 1], "gy"),
            z=remote(r, 3, zs.at[r], zr.at[r], "gz"),
        )

    lane = lax.broadcasted_iota(jnp.int32, (nz, nx), 1)
    row = lax.broadcasted_iota(jnp.int32, (nz, nx), 0)
    half = 2 * ny

    def pack(packed, r, field, y):
        edge = nx - 1 if r % 2 == 0 else 0
        for s in range(2):
            for c in (1, 2):
                column = field[s, c, y][:, edge:edge + 1]
                packed = jnp.where(lane == (2 * s + c - 1) * ny + y, column, packed)
            last = nz - 1 if r % 2 == 0 else 0
            for c in (0, 1):
                zs[r, s, c, y:y + 1] = field[s, c, y, last:last + 1, :]
        return packed

    def rims(r):
        if r % 2 == 0:
            wx, wy, wz, sign = place["gx"] == 0, place["gy"] == 0, place["gz"] == 0, -1.0
        else:
            wx, wy, wz = (place[a] == counts[a] - 1 for a in ("gx", "gy", "gz"))
            sign = 1.0
        cx = jnp.where(wx, math.cos(phase_x), 1.0)
        sx = jnp.where(wx, sign * math.sin(phase_x), 0.0)
        cy = jnp.where(wy, math.cos(phase_y), 1.0)
        sy = jnp.where(wy, sign * math.sin(phase_y), 0.0)
        got = xr[r]
        other = jnp.where(lane < half, -pltpu.roll(got, nx - half, 1), pltpu.roll(got, half, 1))
        return got * cx + other * sx, cy, sy, wz

    def y_rim(r, i, cy, sy):
        a, b = yr[r, i, 0], yr[r, i, 1]
        return (a * cy - b * sy, a * sy + b * cy)

    def beside_x(v, r, packed, s, c, y):
        j = (2 * s + c - 1) * ny + y
        if r % 2 == 0:
            return jnp.where(lane == 0, packed[:, j:j + 1], pltpu.roll(v, 1, 1))
        return jnp.where(lane == nx - 1, packed[:, j:j + 1], pltpu.roll(v, nx - 1, 1))

    def beside_z(v, r, wz, s, c, y):
        rim = jnp.where(wz, 0.0, zr[r, s, c, y:y + 1, :])
        if r % 2 == 0:
            return jnp.where(row == 0, rim, pltpu.roll(v, 1, 0))
        return jnp.where(row == nz - 1, rim, pltpu.roll(v, nz - 1, 0))

    def curl(r, field, y, got, rim):
        packed, _, _, wz = got
        for s in range(2):
            fx, fy, fz = field[s, 0, y], field[s, 1, y], field[s, 2, y]
            if rim is None:
                near = y - 1 if r % 2 == 0 else y + 1
                fx_y, fz_y = field[s, 0, near], field[s, 2, near]
            else:
                fx_y, fz_y = rim[0][s], rim[1][s]
            fx_z = beside_z(fx, r, wz, s, 0, y)
            fy_z = beside_z(fy, r, wz, s, 1, y)
            fy_x = beside_x(fy, r, packed, s, 1, y)
            fz_x = beside_x(fz, r, packed, s, 2, y)
            yield s, 0, (fz - fz_y) - (fy - fy_z)
            yield s, 1, (fx - fx_z) - (fz - fz_x)
            yield s, 2, (fy - fy_x) - (fx - fx_y)

    def update(r, source, target, y, got, rim):
        scale = time_step * inv[y] if r % 2 == 0 else time_step
        for s, c, value in curl(r, source, y, got, rim):
            target[s, c, y] = target[s, c, y] - scale * value

    rounds = 2 * steps
    now = copies(0, h_in)
    now["y0"].start()
    now["y1"].start()
    loads[0].wait()
    packed = jnp.zeros((nz, nx), jnp.float32)
    for y in range(ny):
        packed = pack(packed, 0, h, y)
    xs[0] = packed
    now["x"].start()
    now["z"].start()
    loads[2].wait()
    inverse = [1.0 / jnp.full((nz, nx), eps[m], jnp.float32) for m in range(eps.shape[0])]
    for y in range(ny):
        kind = mat[y]
        value = inverse[0]
        for m in range(1, eps.shape[0]):
            value = jnp.where(kind == m, inverse[m], value)
        inv[y] = value
    loads[1].wait()

    for r in range(rounds):
        source, target = (h, e) if r % 2 == 0 else (e, h)
        inner = range(1, ny) if r % 2 == 0 else range(ny - 1)
        outer = 0 if r % 2 == 0 else ny - 1
        now["x"].wait_recv()
        now["z"].wait_recv()
        got = rims(r)
        packed = jnp.zeros((nz, nx), jnp.float32)
        more = r + 1 < rounds
        for y in inner:
            update(r, source, target, y, got, None)
            if more:
                packed = pack(packed, r + 1, target, y)
        now["y0"].wait_recv()
        now["y1"].wait_recv()
        rim = [y_rim(r, i, got[1], got[2]) for i in range(2)]
        update(r, source, target, outer, got, rim)
        for name in now:
            now[name].wait_send()
        if more:
            now = copies(r + 1, target)
            now["y0"].start()
            now["y1"].start()
            xs[r + 1] = pack(packed, r + 1, target, outer)
            now["x"].start()
            now["z"].start()
        if r % 2 == 0:
            n = r // 2
            if n == 0:
                loads[3].wait()
            for y in range(ny):
                total = None
                for s in range(2):
                    for c in range(3):
                        term = e[s, c, y] * fwd[n, s, c, y].astype(jnp.float32)
                        total = term if total is None else total + term
                total = inv[y] * total
                g[y] = total if n == 0 else g[y] + total


def shards(counts, adj_e, adj_h, fwd_e, material, eps_table):
    ny, nz, nx = material.shape
    rounds = 2 * fwd_e.shape[0]
    hbm = pl.BlockSpec(memory_space=pltpu.HBM)
    vmem = pl.BlockSpec(memory_space=pltpu.VMEM)
    f32 = jnp.float32
    return pl.pallas_call(
        functools.partial(kernel, counts),
        out_shape=(
            pltpu.VMEM(adj_e.shape, f32),
            pltpu.VMEM(adj_h.shape, f32),
            pltpu.VMEM(material.shape, f32),
        ),
        in_specs=[pl.BlockSpec(memory_space=pltpu.SMEM), hbm, hbm, hbm, hbm],
        out_specs=(vmem, vmem, vmem),
        scratch_shapes=[
            pltpu.VMEM(fwd_e.shape, fwd_e.dtype),
            pltpu.VMEM(material.shape, material.dtype),
            pltpu.VMEM(material.shape, f32),
            pltpu.VMEM((rounds, nz, nx), f32),
            pltpu.VMEM((rounds, nz, nx), f32),
            pltpu.VMEM((rounds, 2, 2, nz, nx), f32),
            pltpu.VMEM((rounds, 2, 2, ny, nx), f32),
            pltpu.VMEM((rounds, 2, 2, ny, nx), f32),
            pltpu.SemaphoreType.DMA((4,)),
            pltpu.SemaphoreType.DMA((rounds, 4)),
            pltpu.SemaphoreType.DMA((rounds, 4)),
        ],
        compiler_params=pltpu.CompilerParams(
            collective_id=0, has_side_effects=True, vmem_limit_bytes=24 * 1024 * 1024
        ),
    )(eps_table, adj_e, adj_h, fwd_e, material)


def solution(mesh):
    counts = {a: mesh.shape[a] for a in ("gx", "gy", "gz")}
    return jax.shard_map(
        functools.partial(shards, counts),
        mesh=mesh,
        in_specs=(
            P(None, None, "gy", "gz", "gx"),
            P(None, None, "gy", "gz", "gx"),
            P(None, None, None, "gy", "gz", "gx"),
            P("gy", "gz", "gx"),
            P(),
        ),
        out_specs=(
            P(None, None, "gy", "gz", "gx"),
            P(None, None, "gy", "gz", "gx"),
            P("gy", "gz", "gx"),
        ),
        check_vma=False,
    )
```

```python
import functools
import math

import jax
import jax.numpy as jnp
from jax import lax
from jax.experimental import pallas as pl
from jax.experimental.pallas import tpu as pltpu
from jax.sharding import PartitionSpec as P

time_step = 0.4
phase_x = 1.3
phase_y = 0.7
MESH = pl.DeviceIdType.MESH


def difference(field, s, y, lift, ahead_x, ahead_z):
    fx, fy, fz = field[s, 0, y], field[s, 1, y], field[s, 2, y]
    fx_y, fz_y = lift(s, y)
    return (
        (fz - fz_y) - (fy - ahead_z(fy, s, 1, y)),
        (fx - ahead_z(fx, s, 0, y)) - (fz - ahead_x(fz, s, 2, y)),
        (fy - ahead_x(fy, s, 1, y)) - (fx - fx_y),
    )


def finish(e_in, g_in, h_in, px, ry, rz, e_out, h_out, g_out, h, sem):
    ny, nz, nx = g_in.shape
    out = [pltpu.make_async_copy(e_in, e_out, sem.at[0]), pltpu.make_async_copy(g_in, g_out, sem.at[1])]
    for copy in out:
        copy.start()
    lane = lax.broadcasted_iota(jnp.int32, (nz, nx), 1)
    row = lax.broadcasted_iota(jnp.int32, (nz, nx), 0)
    packed = px[...]

    def lift(s, y):
        if y == ny - 1:
            return ry[0, s], ry[1, s]
        return e_in[s, 0, y + 1], e_in[s, 2, y + 1]

    def ahead_x(v, s, c, y):
        j = (2 * s + c - 1) * ny + y
        return jnp.where(lane == nx - 1, packed[:, j:j + 1], pltpu.roll(v, nx - 1, 1))

    def ahead_z(v, s, c, y):
        return jnp.where(row == nz - 1, rz[s, c, y:y + 1, :], pltpu.roll(v, nz - 1, 0))

    block = ny // 2
    for y in range(ny):
        for s in range(2):
            value = difference(e_in, s, y, lift, ahead_x, ahead_z)
            for c in range(3):
                h[s, c, y] = h_in[s, c, y] - time_step * value[c]
        if (y + 1) % block == 0:
            k = y // block
            layers = pl.ds(k * block, block)
            copy = pltpu.make_async_copy(h.at[:, :, layers], h_out.at[:, :, layers], sem.at[2 + k])
            copy.start()
            out.append(copy)
    for copy in out:
        copy.wait()


def kernel(counts, eps_in, e_in, h_in, fwd_in, mat_in, e, h, g, px, ry, rz,
           eps, fwd, mat, inv, xs, xr, yr, zs, zr, load_sem, send_sem, recv_sem):
    steps = fwd.shape[0]
    ny, nz, nx = mat.shape
    place = {a: lax.axis_index(a) for a in counts}
    after = {a: lax.rem(place[a] + 1, counts[a]) for a in counts}
    before = {a: lax.rem(place[a] + counts[a] - 1, counts[a]) for a in counts}

    loads = [
        pltpu.make_async_copy(h_in, h, load_sem.at[0]),
        pltpu.make_async_copy(e_in, e, load_sem.at[1]),
        pltpu.make_async_copy(mat_in, mat, load_sem.at[2]),
        pltpu.make_async_copy(fwd_in, fwd, load_sem.at[3]),
        pltpu.make_async_copy(eps_in, eps, load_sem.at[4]),
    ]
    for load in loads:
        load.start()

    barrier = pltpu.get_barrier_semaphore()
    greeted = 0
    for a in counts:
        pl.semaphore_signal(barrier, inc=1, device_id={a: after[a]}, device_id_type=MESH)
        greeted += 1
        if counts[a] > 2:
            pl.semaphore_signal(barrier, inc=1, device_id={a: before[a]}, device_id_type=MESH)
            greeted += 1
    pl.semaphore_wait(barrier, greeted)

    def remote(r, which, src, dst, axis):
        to = after[axis] if r % 2 == 0 else before[axis]
        return pltpu.make_async_remote_copy(
            src_ref=src, dst_ref=dst, send_sem=send_sem.at[r, which],
            recv_sem=recv_sem.at[r, which], device_id={axis: to}, device_id_type=MESH)

    def copies(r, field):
        edge = ny - 1 if r % 2 == 0 else 0
        return dict(
            x=remote(r, 0, xs.at[r], xr.at[r], "gx"),
            y0=remote(r, 1, field.at[:, 0, edge], yr.at[r, 0], "gy"),
            y1=remote(r, 2, field.at[:, 2, edge], yr.at[r, 1], "gy"),
            z=remote(r, 3, zs.at[r], zr.at[r], "gz"),
        )

    lane = lax.broadcasted_iota(jnp.int32, (nz, nx), 1)
    row = lax.broadcasted_iota(jnp.int32, (nz, nx), 0)
    half = 2 * ny

    def pack(packed, r, field, y):
        edge = nx - 1 if r % 2 == 0 else 0
        for s in range(2):
            for c in (1, 2):
                column = field[s, c, y][:, edge:edge + 1]
                packed = jnp.where(lane == (2 * s + c - 1) * ny + y, column, packed)
            last = nz - 1 if r % 2 == 0 else 0
            for c in (0, 1):
                zs[r, s, c, y:y + 1] = field[s, c, y, last:last + 1, :]
        return packed

    def rims(r):
        if r % 2 == 0:
            wx, wy, wz, sign = place["gx"] == 0, place["gy"] == 0, place["gz"] == 0, -1.0
        else:
            wx, wy, wz = (place[a] == counts[a] - 1 for a in ("gx", "gy", "gz"))
            sign = 1.0
        cx = jnp.where(wx, math.cos(phase_x), 1.0)
        sx = jnp.where(wx, sign * math.sin(phase_x), 0.0)
        cy = jnp.where(wy, math.cos(phase_y), 1.0)
        sy = jnp.where(wy, sign * math.sin(phase_y), 0.0)
        got = xr[r]
        other = jnp.where(lane < half, -pltpu.roll(got, nx - half, 1), pltpu.roll(got, half, 1))
        return got * cx + other * sx, cy, sy, wz

    def y_rim(r, i, cy, sy):
        a, b = yr[r, i, 0], yr[r, i, 1]
        return (a * cy - b * sy, a * sy + b * cy)

    def beside_x(v, r, packed, s, c, y):
        j = (2 * s + c - 1) * ny + y
        if r % 2 == 0:
            return jnp.where(lane == 0, packed[:, j:j + 1], pltpu.roll(v, 1, 1))
        return jnp.where(lane == nx - 1, packed[:, j:j + 1], pltpu.roll(v, nx - 1, 1))

    def beside_z(v, r, wz, s, c, y):
        rim = jnp.where(wz, 0.0, zr[r, s, c, y:y + 1, :])
        if r % 2 == 0:
            return jnp.where(row == 0, rim, pltpu.roll(v, 1, 0))
        return jnp.where(row == nz - 1, rim, pltpu.roll(v, nz - 1, 0))

    def update(r, source, target, y, got, rim):
        packed, _, _, wz = got
        scale = time_step * inv[y] if r % 2 == 0 else time_step

        def lift(s, y):
            if rim is not None:
                return rim[0][s], rim[1][s]
            near = y - 1 if r % 2 == 0 else y + 1
            return source[s, 0, near], source[s, 2, near]

        def side_x(v, s, c, y):
            return beside_x(v, r, packed, s, c, y)

        def side_z(v, s, c, y):
            return beside_z(v, r, wz, s, c, y)

        for s in range(2):
            value = difference(source, s, y, lift, side_x, side_z)
            for c in range(3):
                target[s, c, y] = target[s, c, y] - scale * value[c]

    rounds = 2 * steps
    now = copies(0, h_in)
    now["y0"].start()
    now["y1"].start()
    loads[0].wait()
    packed = jnp.zeros((nz, nx), jnp.float32)
    for y in range(ny):
        packed = pack(packed, 0, h, y)
    xs[0] = packed
    now["x"].start()
    now["z"].start()
    loads[2].wait()
    loads[4].wait()
    inverse = [1.0 / jnp.full((nz, nx), eps[m], jnp.float32) for m in range(eps.shape[0])]
    for y in range(ny):
        kind = mat[y]
        value = inverse[0]
        for m in range(1, eps.shape[0]):
            value = jnp.where(kind == m, inverse[m], value)
        inv[y] = value
    loads[1].wait()

    for r in range(rounds):
        source, target = (h, e) if r % 2 == 0 else (e, h)
        inner = range(1, ny) if r % 2 == 0 else range(ny - 1)
        outer = 0 if r % 2 == 0 else ny - 1
        now["x"].wait_recv()
        now["z"].wait_recv()
        got = rims(r)
        if r == rounds - 1:
            px[...] = got[0]
            for s in range(2):
                for c in range(2):
                    rz[s, c] = jnp.where(got[3], 0.0, zr[r, s, c])
            now["y0"].wait_recv()
            now["y1"].wait_recv()
            for i in range(2):
                ry[i, 0], ry[i, 1] = y_rim(r, i, got[1], got[2])
            for name in now:
                now[name].wait_send()
            break
        packed = jnp.zeros((nz, nx), jnp.float32)
        for y in inner:
            update(r, source, target, y, got, None)
            packed = pack(packed, r + 1, target, y)
        now["y0"].wait_recv()
        now["y1"].wait_recv()
        rim = [y_rim(r, i, got[1], got[2]) for i in range(2)]
        update(r, source, target, outer, got, rim)
        for name in now:
            now[name].wait_send()
        now = copies(r + 1, target)
        now["y0"].start()
        now["y1"].start()
        xs[r + 1] = pack(packed, r + 1, target, outer)
        now["x"].start()
        now["z"].start()
        if r % 2 == 0:
            n = r // 2
            if n == 0:
                loads[3].wait()
            for y in range(ny):
                total = None
                for s in range(2):
                    for c in range(3):
                        term = e[s, c, y] * fwd[n, s, c, y].astype(jnp.float32)
                        total = term if total is None else total + term
                total = inv[y] * total
                g[y] = total if n == 0 else g[y] + total


def shards(counts, adj_e, adj_h, fwd_e, material, eps_table):
    ny, nz, nx = material.shape
    rounds = 2 * fwd_e.shape[0]
    hbm = pl.BlockSpec(memory_space=pltpu.HBM)
    vmem = pl.BlockSpec(memory_space=pltpu.VMEM)
    f32 = jnp.float32
    e, h, g, px, ry, rz = pl.pallas_call(
        functools.partial(kernel, counts),
        out_shape=(
            pltpu.VMEM(adj_e.shape, f32),
            pltpu.VMEM(adj_h.shape, f32),
            pltpu.VMEM(material.shape, f32),
            pltpu.VMEM((nz, nx), f32),
            pltpu.VMEM((2, 2, nz, nx), f32),
            pltpu.VMEM((2, 2, ny, nx), f32),
        ),
        in_specs=[hbm] * 5,
        out_specs=[vmem] * 6,
        scratch_shapes=[
            pltpu.SMEM(eps_table.shape, f32),
            pltpu.VMEM(fwd_e.shape, fwd_e.dtype),
            pltpu.VMEM(material.shape, material.dtype),
            pltpu.VMEM(material.shape, f32),
            pltpu.VMEM((rounds, nz, nx), f32),
            pltpu.VMEM((rounds, nz, nx), f32),
            pltpu.VMEM((rounds, 2, 2, nz, nx), f32),
            pltpu.VMEM((rounds, 2, 2, ny, nx), f32),
            pltpu.VMEM((rounds, 2, 2, ny, nx), f32),
            pltpu.SemaphoreType.DMA((5,)),
            pltpu.SemaphoreType.DMA((rounds, 4)),
            pltpu.SemaphoreType.DMA((rounds, 4)),
        ],
        compiler_params=pltpu.CompilerParams(
            collective_id=0, has_side_effects=True, vmem_limit_bytes=24 * 1024 * 1024
        ),
    )(*(pltpu.with_memory_space_constraint(a, pltpu.HBM) for a in (eps_table, adj_e, adj_h, fwd_e, material)))
    return pl.pallas_call(
        finish,
        out_shape=(
            jax.ShapeDtypeStruct(adj_e.shape, f32),
            jax.ShapeDtypeStruct(adj_h.shape, f32),
            jax.ShapeDtypeStruct(material.shape, f32),
        ),
        in_specs=[vmem] * 6,
        out_specs=[hbm] * 3,
        scratch_shapes=[pltpu.VMEM(adj_h.shape, f32), pltpu.SemaphoreType.DMA((4,))],
        compiler_params=pltpu.CompilerParams(vmem_limit_bytes=8 * 1024 * 1024),
    )(e, g, h, px, ry, rz)


def solution(mesh):
    counts = {a: mesh.shape[a] for a in ("gx", "gy", "gz")}
    return jax.shard_map(
        functools.partial(shards, counts),
        mesh=mesh,
        in_specs=(
            P(None, None, "gy", "gz", "gx"),
            P(None, None, "gy", "gz", "gx"),
            P(None, None, None, "gy", "gz", "gx"),
            P("gy", "gz", "gx"),
            P(),
        ),
        out_specs=(
            P(None, None, "gy", "gz", "gx"),
            P(None, None, "gy", "gz", "gx"),
            P("gy", "gz", "gx"),
        ),
        check_vma=False,
    )
```

```python
import functools
import math

import jax
import jax.numpy as jnp
from jax import lax
from jax.experimental import pallas as pl
from jax.experimental.pallas import tpu as pltpu
from jax.sharding import PartitionSpec as P

time_step = 0.4
phase_x = 1.3
phase_y = 0.7
MESH = pl.DeviceIdType.MESH


def difference(field, s, y, lift, ahead_x, ahead_z):
    fx, fy, fz = field[s, 0, y], field[s, 1, y], field[s, 2, y]
    fx_y, fz_y = lift(s, y)
    return (
        (fz - fz_y) - (fy - ahead_z(fy, s, 1, y)),
        (fx - ahead_z(fx, s, 0, y)) - (fz - ahead_x(fz, s, 2, y)),
        (fy - ahead_x(fy, s, 1, y)) - (fx - fx_y),
    )


def finish(e_in, g_in, h_in, px, ry, rz, e_out, h_out, g_out, h, sem):
    ny, nz, nx = g_in.shape
    out = [pltpu.make_async_copy(e_in, e_out, sem.at[0]), pltpu.make_async_copy(g_in, g_out, sem.at[1])]
    for copy in out:
        copy.start()
    lane = lax.broadcasted_iota(jnp.int32, (nz, nx), 1)
    row = lax.broadcasted_iota(jnp.int32, (nz, nx), 0)

    def lift(s, y):
        if y == ny - 1:
            return ry[0, s], ry[1, s]
        return e_in[s, 0, y + 1], e_in[s, 2, y + 1]

    def ahead_x(v, s, c, y):
        j = s * ny + y
        return jnp.where(lane == nx - 1, px[c - 1][:, j:j + 1], pltpu.roll(v, nx - 1, 1))

    def ahead_z(v, s, c, y):
        return jnp.where(row == nz - 1, rz[s, c, y:y + 1, :], pltpu.roll(v, nz - 1, 0))

    block = ny // 2
    for y in range(ny):
        for s in range(2):
            value = difference(e_in, s, y, lift, ahead_x, ahead_z)
            for c in range(3):
                h[s, c, y] = h_in[s, c, y] - time_step * value[c]
        if (y + 1) % block == 0:
            k = y // block
            layers = pl.ds(k * block, block)
            copy = pltpu.make_async_copy(h.at[:, :, layers], h_out.at[:, :, layers], sem.at[2 + k])
            copy.start()
            out.append(copy)
    for copy in out:
        copy.wait()


FACES = (
    ("xp", (1, 0, 0)), ("xm", (-1, 0, 0)), ("yp0", (0, 1, 0)), ("yp2", (0, 1, 0)),
    ("ym", (0, -1, 0)), ("zp", (0, 0, 1)), ("zm", (0, 0, -1)),
)
EDGES = (
    ("ymzp", (0, -1, 1)), ("ymxp", (1, -1, 0)), ("xmzp", (-1, 0, 1)),
    ("xmyp", (-1, 1, 0)), ("zmyp", (0, 1, -1)), ("zmxp", (1, 0, -1)),
)
FIRST = (
    ("ey0", (0, -1, 0)), ("ey2", (0, -1, 0)), ("em", (0, -1, 0)), ("ex", (-1, 0, 0)), ("ez", (0, 0, -1)),
)
SENDS = FACES + EDGES + FIRST


def kernel(counts, eps_in, e_in, h_in, fwd_in, mat_in, e, h, g, px, ry, rz,
           eps, fwd, mat, inv, kx, ky, kz,
           xp, xp_s, xm_s, ed, zp, zm, xp_r, xm_r, yp_r, ym_r, zp_r, zm_r,
           ymzp_r, ymxp_r, xmzp_r, xmyp_r, zmyp_r, zmxp_r,
           ex, ez, ex_r, ey_r, em_r, ez_r, load_sem, send_sem, recv_sem):
    steps = fwd.shape[0]
    ny, nz, nx = mat.shape
    axes = ("gx", "gy", "gz")
    place = {a: lax.axis_index(a) for a in axes}

    def at(offset):
        return {a: lax.rem(place[a] + (o % counts[a]), counts[a]) for a, o in zip(axes, offset)}

    near = []
    for _, offset in FACES + EDGES:
        for sign in (1, -1):
            o = tuple(sign * v % counts[a] for a, v in zip(axes, offset))
            if o not in near and any(o):
                near.append(o)
    barrier = pltpu.get_barrier_semaphore()
    for o in near:
        pl.semaphore_signal(barrier, inc=1, device_id=at(o), device_id_type=MESH)
    loads = [
        pltpu.make_async_copy(h_in, h, load_sem.at[0]),
        pltpu.make_async_copy(e_in, e, load_sem.at[1]),
        pltpu.make_async_copy(mat_in, mat, load_sem.at[2]),
        pltpu.make_async_copy(eps_in, eps, load_sem.at[4]),
        pltpu.make_async_copy(fwd_in, fwd, load_sem.at[3]),
    ]
    for load in loads:
        load.start()
    load_h, load_e, load_mat, load_eps, load_fwd = loads

    pl.semaphore_wait(barrier, len(near))

    def copies(n):
        field = h_in if n == 0 else h
        ends = dict(
            xp=(xp_s.at[n], xp_r.at[n]),
            xm=(xm_s.at[n], xm_r.at[n]),
            yp0=(field.at[:, 0, ny - 1], yp_r.at[n, 0]),
            yp2=(field.at[:, 2, ny - 1], yp_r.at[n, 1]),
            ym=(field.at[:, :, 0], ym_r.at[n]),
            zp=(zp.at[n], zp_r.at[n]),
            zm=(zm.at[n], zm_r.at[n]),
            ymzp=(ed.at[n], ymzp_r.at[n]),
            ymxp=(xp_s.at[n], ymxp_r.at[n]),
            xmzp=(xm_s.at[n, 1], xmzp_r.at[n]),
            xmyp=(xm_s.at[n, 1], xmyp_r.at[n]),
            zmyp=(ed.at[n], zmyp_r.at[n]),
            zmxp=(xp_s.at[n], zmxp_r.at[n]),
        )
        if n == 0:
            ends.update(
                ey0=(e_in.at[:, 0, 0], ey_r.at[0]),
                ey2=(e_in.at[:, 2, 0], ey_r.at[1]),
                em=(mat_in.at[0], em_r),
                ex=(ex, ex_r),
                ez=(ez, ez_r),
            )
        return {
            name: pltpu.make_async_remote_copy(
                src_ref=ends[name][0], dst_ref=ends[name][1], send_sem=send_sem.at[n, i],
                recv_sem=recv_sem.at[n, i], device_id=at(offset), device_id_type=MESH)
            for i, (name, offset) in enumerate(SENDS) if name in ends
        }

    lane = lax.broadcasted_iota(jnp.int32, (nz, nx), 1)
    row = lax.broadcasted_iota(jnp.int32, (nz, nx), 0)
    lane8, row8 = lane[:ny], row[:ny]
    blank = jnp.zeros((nz, nx), jnp.float32)

    def turn(axis, place_of_wrap, phase):
        wraps = place[axis] == place_of_wrap
        return jnp.where(wraps, math.cos(phase), 1.0), jnp.where(wraps, math.sin(phase), 0.0)

    x_behind, x_ahead = turn("gx", 0, -phase_x), turn("gx", counts["gx"] - 1, phase_x)
    y_behind, y_ahead = turn("gy", 0, -phase_y), turn("gy", counts["gy"] - 1, phase_y)
    z_first, z_last = place["gz"] == 0, place["gz"] == counts["gz"] - 1

    def rot(a, b, by):
        return a * by[0] - b * by[1], a * by[1] + b * by[0]

    def rot_packed(v, by):
        index = lax.broadcasted_iota(jnp.int32, v.shape, 1)
        other = jnp.where(index < ny, -pltpu.roll(v, nx - ny, 1), pltpu.roll(v, ny, 1))
        return v * by[0] + other * by[1]

    tiles = nz // 8
    width = nx // tiles

    def fold(a, b):
        v = a if b is None else a + pltpu.roll(b, 2 * ny, 1)
        total = v[0:8]
        for k in range(1, tiles):
            total = total + pltpu.roll(v[8 * k:8 * k + 8], k * width, 1)
        return total

    def unfold(v):
        a = jnp.concatenate([v] + [pltpu.roll(v, nx - k * width, 1) for k in range(1, tiles)], 0)
        return a, pltpu.roll(a, nx - 2 * ny, 1)

    def put(packed, column, y, s):
        return jnp.where(lane == s * ny + y, column, packed)

    def pack(packed, n, y):
        packed = list(packed)
        for s in range(2):
            for c in range(3):
                v = h[s, c, y]
                if c > 0:
                    packed[c - 1] = put(packed[c - 1], v[:, nx - 1:nx], y, s)
                packed[2 + c] = put(packed[2 + c], v[:, 0:1], y, s)
                if c < 2:
                    zp[n, s, c, y:y + 1] = h[s, c, y, nz - 1:nz, :]
                zm[n, s, c, y:y + 1] = h[s, c, y, 0:1, :]
        return packed

    def store_packed(packed, n):
        for i in range(2):
            xp[n, i] = packed[i]
        xp_s[n] = fold(packed[0], packed[1])
        xm_s[n, 0] = fold(packed[3], packed[4])
        xm_s[n, 1] = fold(packed[2], None)
        for s in range(2):
            ed[n, s:s + 1] = h[s, 1, 0, nz - 1:nz, :]
            ed[n, 2 + s:3 + s] = h[s, 2, ny - 1, 0:1, :]
        ed[n, 4:8] = jnp.zeros((4, nx), jnp.float32)

    def start(now, *names):
        for name in names:
            now[name].start()

    def landed(now, *names):
        for name in names:
            now[name].wait_recv()

    def shift(v, before, axis):
        index = lax.broadcasted_iota(jnp.int32, v.shape, axis)
        return jnp.where(index == 0, before, pltpu.roll(v, 1, axis))

    def update_e(n, y, xb, yb):
        scale = time_step * inv[y]

        def lift(s, y):
            if yb is not None:
                return yb[0][s], yb[1][s]
            return h[s, 0, y - 1], h[s, 2, y - 1]

        def side_x(v, s, c, y):
            j = s * ny + y
            return shift(v, xb[c - 1][:, j:j + 1], 1)

        def side_z(v, s, c, y):
            return shift(v, jnp.where(z_first, 0.0, zp_r[n, s, c, y:y + 1, :]), 0)

        for s in range(2):
            value = difference(h, s, y, lift, side_x, side_z)
            for c in range(3):
                e[s, c, y] = e[s, c, y] - scale * value[c]

    def update_h(y):
        def lift(s, y):
            if y == ny - 1:
                return ry[0, s], ry[1, s]
            return e[s, 0, y + 1], e[s, 2, y + 1]

        def side_x(v, s, c, y):
            j = s * ny + y
            return jnp.where(lane == nx - 1, px[c - 1][:, j:j + 1], pltpu.roll(v, nx - 1, 1))

        def side_z(v, s, c, y):
            return jnp.where(row == nz - 1, rz[s, c, y:y + 1, :], pltpu.roll(v, nz - 1, 0))

        for s in range(2):
            value = difference(e, s, y, lift, side_x, side_z)
            for c in range(3):
                h[s, c, y] = h[s, c, y] + -time_step * value[c]

    def front_x(n):
        hx, hy, hz = (rot_packed(v, x_ahead) for v in (unfold(xm_r[n, 1])[0], *unfold(xm_r[n, 0])))
        below = jnp.where(z_first, 0.0, rot_packed(unfold(xmzp_r[n])[0], x_ahead)[nz - 1:nz, :])
        hx_z = shift(hx, below, 0)
        side = rot_packed(rot_packed(unfold(xmyp_r[n])[0], x_ahead), y_behind)
        side = pltpu.roll(side, nx - (ny - 1), 1)
        first = jnp.logical_or(lane == 0, lane == ny)
        hx_y = jnp.where(first, side, pltpu.roll(hx, 1, 1))
        scale = time_step * kx[...]
        px[0] = px[0] - scale * ((hx - hx_z) - (hz - xp[n, 1]))
        px[1] = px[1] - scale * ((hy - xp[n, 0]) - (hx - hx_y))

    def front_z(n):
        scale = time_step * kz[...]
        side = rot(zmyp_r[n, 2:3, :], zmyp_r[n, 3:4, :], y_behind)
        corner = rot_packed(unfold(zmxp_r[n])[1], x_behind)[0:1, :]
        for s in range(2):
            hx, hy, hz = (zm_r[n, s, c] for c in range(3))
            hz_y = shift(hz, side[s], 0)
            column = jnp.sum(jnp.where(lane8 == s * ny + row8, corner, 0.0), axis=1, keepdims=True)
            hz_x = shift(hz, column, 1)
            e_x = rz[s, 0] - scale * ((hz - hz_y) - (hy - zp[n, s, 1]))
            e_y = rz[s, 1] - scale * ((hx - zp[n, s, 0]) - (hz - hz_x))
            rz[s, 0] = jnp.where(z_last, 0.0, e_x)
            rz[s, 1] = jnp.where(z_last, 0.0, e_y)

    def front_y(n):
        scale = time_step * ky[...]
        ahead = [rot(ym_r[n, 0, c], ym_r[n, 1, c], y_ahead) for c in range(3)]
        below = rot(ymzp_r[n, 0:1, :], ymzp_r[n, 1:2, :], y_ahead)
        corner = rot_packed(rot_packed(unfold(ymxp_r[n])[0], y_ahead), x_behind)
        for s in range(2):
            hx, hy, hz = (ahead[c][s] for c in range(3))
            hy_z = shift(hy, jnp.where(z_first, 0.0, below[s]), 0)
            hy_x = shift(hy, corner[:, s * ny:s * ny + 1], 1)
            ry[0, s] = ry[0, s] - scale * ((hz - h[s, 2, ny - 1]) - (hy - hy_z))
            ry[1, s] = ry[1, s] - scale * ((hy - hy_x) - (hx - h[s, 0, ny - 1]))

    def gradient(n):
        for y in range(ny):
            total = None
            for s in range(2):
                for c in range(3):
                    term = e[s, c, y] * fwd[n, s, c, y].astype(jnp.float32)
                    total = term if total is None else total + term
            total = inv[y] * total
            g[y] = total if n == 0 else g[y] + total

    now = copies(0)
    start(now, "yp0", "yp2", "ym", "em", "ey0", "ey2")
    load_h.wait()
    packed = [blank] * 5
    for y in range(ny):
        packed = pack(packed, 0, y)
    store_packed(packed, 0)
    start(now, "xp", "zp", "xm", "zm")
    start(now, *(name for name, _ in EDGES))
    load_mat.wait()
    load_eps.wait()
    table = [1.0 / jnp.full((nz, nx), eps[m], jnp.float32) for m in range(eps.shape[0])]

    def inverse(kind):
        value = table[0]
        for m in range(1, eps.shape[0]):
            value = jnp.where(kind == m, table[m], value)
        return value

    for y in range(ny):
        inv[y] = inverse(mat[y])
    load_e.wait()
    packed = [blank] * 3
    for y in range(ny):
        for s in range(2):
            for c in (1, 2):
                packed[c - 1] = put(packed[c - 1], e[s, c, y][:, 0:1], y, s)
            packed[2] = put(packed[2], inv[y][:, 0:1], y, s)
            for c in (0, 1):
                ez[2 * s + c, y:y + 1] = e[s, c, y, 0:1, :]
        ez[4, y:y + 1] = inv[y, 0:1, :]
    ex[0] = fold(packed[0], packed[1])
    ex[1] = fold(packed[2], None)
    start(now, "ex", "ez")

    for n in range(steps):
        landed(now, "xp", "zp")
        xb = [rot_packed(v, x_behind) for v in unfold(xp_r[n])]
        for y in range(1, ny):
            update_e(n, y, xb, None)
        landed(now, "yp0", "yp2")
        update_e(n, 0, xb, [rot(yp_r[n, i, 0], yp_r[n, i, 1], y_behind) for i in range(2)])
        if n == steps - 1:
            if n == 0:
                load_fwd.wait()
            gradient(n)
        if n == 0:
            landed(now, "ex", "ez", "em", "ey0", "ey2")
            ex_u = unfold(ex_r[0])
            for i in range(2):
                px[i] = rot_packed(ex_u[i], x_ahead)
                ry[i, 0], ry[i, 1] = rot(ey_r[i, 0], ey_r[i, 1], y_ahead)
                for c in range(2):
                    rz[i, c] = ez_r[2 * i + c]
            kx[...] = unfold(ex_r[1])[0]
            kz[...] = ez_r[4]
            ky[...] = inverse(em_r[...])
        landed(now, "xm", "zm", *(name for name, _ in EDGES))
        front_x(n)
        front_z(n)
        landed(now, "ym")
        front_y(n)
        for copy in now.values():
            copy.wait_send()
        if n == steps - 1:
            break
        packed = [blank] * 5
        later = copies(n + 1)
        for y in (0, ny - 1, *range(1, ny - 1)):
            update_h(y)
            packed = pack(packed, n + 1, y)
            if y == 0:
                later["ym"].start()
            if y == ny - 1:
                start(later, "yp0", "yp2")
        store_packed(packed, n + 1)
        start(later, "xp", "zp", "xm", "zm")
        start(later, *(name for name, _ in EDGES))
        now = later
        if n == 0:
            load_fwd.wait()
        gradient(n)


def shards(counts, adj_e, adj_h, fwd_e, material, eps_table):
    ny, nz, nx = material.shape
    steps = fwd_e.shape[0]
    hbm = pl.BlockSpec(memory_space=pltpu.HBM)
    vmem = pl.BlockSpec(memory_space=pltpu.VMEM)
    f32 = jnp.float32
    e, h, g, px, ry, rz = pl.pallas_call(
        functools.partial(kernel, counts),
        out_shape=(
            pltpu.VMEM(adj_e.shape, f32),
            pltpu.VMEM(adj_h.shape, f32),
            pltpu.VMEM(material.shape, f32),
            pltpu.VMEM((2, nz, nx), f32),
            pltpu.VMEM((2, 2, nz, nx), f32),
            pltpu.VMEM((2, 2, ny, nx), f32),
        ),
        in_specs=[hbm] * 5,
        out_specs=[vmem] * 6,
        scratch_shapes=[
            pltpu.SMEM(eps_table.shape, f32),
            pltpu.VMEM(fwd_e.shape, fwd_e.dtype),
            pltpu.VMEM(material.shape, material.dtype),
            pltpu.VMEM(material.shape, f32),
            pltpu.VMEM((nz, nx), f32),
            pltpu.VMEM((nz, nx), f32),
            pltpu.VMEM((ny, nx), f32),
            *(pltpu.VMEM((steps, *shape), f32) for shape in (
                (2, nz, nx), (8, nx), (2, 8, nx), (8, nx), (2, 2, ny, nx), (2, 3, ny, nx),
                (8, nx), (2, 8, nx), (2, 2, nz, nx), (2, 3, nz, nx),
                (2, 2, ny, nx), (2, 3, ny, nx), *[(8, nx)] * 6)),
            pltpu.VMEM((2, 8, nx), f32),
            pltpu.VMEM((5, ny, nx), f32),
            pltpu.VMEM((2, 8, nx), f32),
            pltpu.VMEM((2, 2, nz, nx), f32),
            pltpu.VMEM((nz, nx), material.dtype),
            pltpu.VMEM((5, ny, nx), f32),
            pltpu.SemaphoreType.DMA((5,)),
            pltpu.SemaphoreType.DMA((steps, len(SENDS))),
            pltpu.SemaphoreType.DMA((steps, len(SENDS))),
        ],
        compiler_params=pltpu.CompilerParams(
            collective_id=0, has_side_effects=True, vmem_limit_bytes=24 * 1024 * 1024
        ),
    )(*(pltpu.with_memory_space_constraint(a, pltpu.HBM) for a in (eps_table, adj_e, adj_h, fwd_e, material)))
    return pl.pallas_call(
        finish,
        out_shape=(
            jax.ShapeDtypeStruct(adj_e.shape, f32),
            jax.ShapeDtypeStruct(adj_h.shape, f32),
            jax.ShapeDtypeStruct(material.shape, f32),
        ),
        in_specs=[vmem] * 6,
        out_specs=[hbm] * 3,
        scratch_shapes=[pltpu.VMEM(adj_h.shape, f32), pltpu.SemaphoreType.DMA((4,))],
        compiler_params=pltpu.CompilerParams(vmem_limit_bytes=8 * 1024 * 1024),
    )(e, g, h, px, ry, rz)


def solution(mesh):
    counts = {a: mesh.shape[a] for a in ("gx", "gy", "gz")}
    return jax.shard_map(
        functools.partial(shards, counts),
        mesh=mesh,
        in_specs=(
            P(None, None, "gy", "gz", "gx"),
            P(None, None, "gy", "gz", "gx"),
            P(None, None, None, "gy", "gz", "gx"),
            P("gy", "gz", "gx"),
            P(),
        ),
        out_specs=(
            P(None, None, "gy", "gz", "gx"),
            P(None, None, "gy", "gz", "gx"),
            P("gy", "gz", "gx"),
        ),
        check_vma=False,
    )
```

```python
import functools
import math

import jax
import jax.numpy as jnp
from jax import lax
from jax.experimental import pallas as pl
from jax.experimental.pallas import tpu as pltpu
from jax.sharding import PartitionSpec as P

time_step = 0.4
phase_x = 1.3
phase_y = 0.7
MESH = pl.DeviceIdType.MESH


def difference(field, s, y, lift, ahead_x, ahead_z):
    fx, fy, fz = field[s, 0, y], field[s, 1, y], field[s, 2, y]
    fx_y, fz_y = lift(s, y)
    return (
        (fz - fz_y) - (fy - ahead_z(fy, s, 1, y)),
        (fx - ahead_z(fx, s, 0, y)) - (fz - ahead_x(fz, s, 2, y)),
        (fy - ahead_x(fy, s, 1, y)) - (fx - fx_y),
    )


def finish(e_in, g_in, h_in, px, ry, rz, e_out, h_out, g_out, h, sem):
    ny, nz, nx = g_in.shape
    out = [pltpu.make_async_copy(e_in, e_out, sem.at[0]), pltpu.make_async_copy(g_in, g_out, sem.at[1])]
    for copy in out:
        copy.start()
    lane = lax.broadcasted_iota(jnp.int32, (nz, nx), 1)
    row = lax.broadcasted_iota(jnp.int32, (nz, nx), 0)

    def lift(s, y):
        if y == ny - 1:
            return ry[0, s], ry[1, s]
        return e_in[s, 0, y + 1], e_in[s, 2, y + 1]

    def ahead_x(v, s, c, y):
        j = s * ny + y
        return jnp.where(lane == nx - 1, px[c - 1][:, j:j + 1], pltpu.roll(v, nx - 1, 1))

    def ahead_z(v, s, c, y):
        return jnp.where(row == nz - 1, rz[s, c, y:y + 1, :], pltpu.roll(v, nz - 1, 0))

    block = ny // 2
    for y in range(ny):
        for s in range(2):
            value = difference(e_in, s, y, lift, ahead_x, ahead_z)
            for c in range(3):
                h[s, c, y] = h_in[s, c, y] - time_step * value[c]
        if (y + 1) % block == 0:
            k = y // block
            layers = pl.ds(k * block, block)
            copy = pltpu.make_async_copy(h.at[:, :, layers], h_out.at[:, :, layers], sem.at[2 + k])
            copy.start()
            out.append(copy)
    for copy in out:
        copy.wait()


FACES = (
    ("xp", (1, 0, 0)), ("xm", (-1, 0, 0)), ("yp0", (0, 1, 0)), ("yp2", (0, 1, 0)),
    ("ym", (0, -1, 0)), ("zp", (0, 0, 1)), ("zm", (0, 0, -1)),
)
EDGES = (
    ("ymzp", (0, -1, 1)), ("ymxp", (1, -1, 0)), ("xmzp", (-1, 0, 1)),
    ("xmyp", (-1, 1, 0)), ("zmyp", (0, 1, -1)), ("zmxp", (1, 0, -1)),
)
FIRST = (
    ("em", (0, -1, 0)), ("ex", (-1, 0, 0)), ("ez", (0, 0, -1)),
)
SENDS = FACES + EDGES + FIRST


def kernel(counts, eps_in, e_in, h_in, fwd_in, mat_in, e, h, g, px, ry, rz,
           eps, fwd, mat, inv, kx, ky, kz,
           xp, xp_s, xm_s, ed, zp, zm, xp_r, xm_r, yp_r, ym_r, zp_r, zm_r,
           ymzp_r, ymxp_r, xmzp_r, xmyp_r, zmyp_r, zmxp_r,
           ex, ez, ex_r, ys, em_r, ez_r, load_sem, send_sem, recv_sem):
    steps = fwd.shape[0]
    ny, nz, nx = mat.shape
    axes = ("gx", "gy", "gz")
    place = {a: lax.axis_index(a) for a in axes}

    def at(offset):
        return {a: lax.rem(place[a] + (o % counts[a]), counts[a]) for a, o in zip(axes, offset)}

    near = []
    for _, offset in FACES + EDGES:
        for sign in (1, -1):
            o = tuple(sign * v % counts[a] for a, v in zip(axes, offset))
            if o not in near and any(o):
                near.append(o)
    barrier = pltpu.get_barrier_semaphore()
    for o in near:
        pl.semaphore_signal(barrier, inc=1, device_id=at(o), device_id_type=MESH)
    loads = [
        pltpu.make_async_copy(h_in, h, load_sem.at[0]),
        pltpu.make_async_copy(e_in, e, load_sem.at[1]),
        pltpu.make_async_copy(mat_in, mat, load_sem.at[2]),
        pltpu.make_async_copy(eps_in, eps, load_sem.at[4]),
        pltpu.make_async_copy(fwd_in, fwd, load_sem.at[3]),
    ]
    for load in loads:
        load.start()
    load_h, load_e, load_mat, load_eps, load_fwd = loads

    pl.semaphore_wait(barrier, len(near))

    def copies(n):
        field = h_in if n == 0 else h
        ends = dict(
            xp=(xp_s.at[n], xp_r.at[n]),
            xm=(xm_s.at[n], xm_r.at[n]),
            yp0=(field.at[:, 0, ny - 1], yp_r.at[n, 0]),
            yp2=(field.at[:, 2, ny - 1], yp_r.at[n, 1]),
            ym=(ys.at[n], ym_r.at[n]),
            zp=(zp.at[n], zp_r.at[n]),
            zm=(zm.at[n], zm_r.at[n]),
            ymzp=(ed.at[n], ymzp_r.at[n]),
            ymxp=(xp_s.at[n], ymxp_r.at[n]),
            xmzp=(xm_s.at[n, 1], xmzp_r.at[n]),
            xmyp=(xm_s.at[n, 1], xmyp_r.at[n]),
            zmyp=(ed.at[n], zmyp_r.at[n]),
            zmxp=(xp_s.at[n], zmxp_r.at[n]),
        )
        if n == 0:
            ends.update(
                em=(mat_in.at[0], em_r),
                ex=(ex, ex_r),
                ez=(ez, ez_r),
            )
        return {
            name: pltpu.make_async_remote_copy(
                src_ref=ends[name][0], dst_ref=ends[name][1], send_sem=send_sem.at[n, i],
                recv_sem=recv_sem.at[n, i], device_id=at(offset), device_id_type=MESH)
            for i, (name, offset) in enumerate(SENDS) if name in ends
        }

    lane = lax.broadcasted_iota(jnp.int32, (nz, nx), 1)
    row = lax.broadcasted_iota(jnp.int32, (nz, nx), 0)
    lane8, row8 = lane[:ny], row[:ny]
    blank = jnp.zeros((nz, nx), jnp.float32)

    def turn(axis, place_of_wrap, phase):
        wraps = place[axis] == place_of_wrap
        return jnp.where(wraps, math.cos(phase), 1.0), jnp.where(wraps, math.sin(phase), 0.0)

    x_behind, x_ahead = turn("gx", 0, -phase_x), turn("gx", counts["gx"] - 1, phase_x)
    y_behind, y_ahead = turn("gy", 0, -phase_y), turn("gy", counts["gy"] - 1, phase_y)
    z_first, z_last = place["gz"] == 0, place["gz"] == counts["gz"] - 1

    def rot(a, b, by):
        return a * by[0] - b * by[1], a * by[1] + b * by[0]

    def rot_packed(v, by):
        index = lax.broadcasted_iota(jnp.int32, v.shape, 1)
        other = jnp.where(index < ny, -pltpu.roll(v, nx - ny, 1), pltpu.roll(v, ny, 1))
        return v * by[0] + other * by[1]

    tiles = nz // 8
    width = nx // tiles

    def fold(a, b):
        v = a if b is None else a + pltpu.roll(b, 2 * ny, 1)
        total = v[0:8]
        for k in range(1, tiles):
            total = total + pltpu.roll(v[8 * k:8 * k + 8], k * width, 1)
        return total

    def unfold(v):
        a = jnp.concatenate([v] + [pltpu.roll(v, nx - k * width, 1) for k in range(1, tiles)], 0)
        return a, pltpu.roll(a, nx - 2 * ny, 1)

    def put(packed, column, y, s):
        return jnp.where(lane == s * ny + y, column, packed)

    def pack(packed, n, y):
        packed = list(packed)
        for s in range(2):
            for c in range(3):
                v = h[s, c, y]
                if c > 0:
                    packed[c - 1] = put(packed[c - 1], v[:, nx - 1:nx], y, s)
                packed[2 + c] = put(packed[2 + c], v[:, 0:1], y, s)
                if c < 2:
                    zp[n, s, c, y:y + 1] = h[s, c, y, nz - 1:nz, :]
                zm[n, s, c, y:y + 1] = h[s, c, y, 0:1, :]
        return packed

    def store_packed(packed, n):
        for i in range(2):
            xp[n, i] = packed[i]
        xp_s[n] = fold(packed[0], packed[1])
        xm_s[n, 0] = fold(packed[3], packed[4])
        xm_s[n, 1] = fold(packed[2], None)
        for s in range(2):
            ed[n, s:s + 1] = h[s, 1, 0, nz - 1:nz, :]
            ed[n, 2 + s:3 + s] = h[s, 2, ny - 1, 0:1, :]
        ed[n, 4:8] = jnp.zeros((4, nx), jnp.float32)

    def start(now, *names):
        for name in names:
            now[name].start()

    def landed(now, *names):
        for name in names:
            now[name].wait_recv()

    def shift(v, before, axis):
        index = lax.broadcasted_iota(jnp.int32, v.shape, axis)
        return jnp.where(index == 0, before, pltpu.roll(v, 1, axis))

    def update_e(n, y, xb, yb):
        scale = time_step * inv[y]

        def lift(s, y):
            if yb is not None:
                return yb[0][s], yb[1][s]
            return h[s, 0, y - 1], h[s, 2, y - 1]

        def side_x(v, s, c, y):
            j = s * ny + y
            return shift(v, xb[c - 1][:, j:j + 1], 1)

        def side_z(v, s, c, y):
            return shift(v, jnp.where(z_first, 0.0, zp_r[n, s, c, y:y + 1, :]), 0)

        for s in range(2):
            value = difference(h, s, y, lift, side_x, side_z)
            for c in range(3):
                e[s, c, y] = e[s, c, y] - scale * value[c]

    def update_h(y):
        def lift(s, y):
            if y == ny - 1:
                return ry[0, s], ry[1, s]
            return e[s, 0, y + 1], e[s, 2, y + 1]

        def side_x(v, s, c, y):
            j = s * ny + y
            return jnp.where(lane == nx - 1, px[c - 1][:, j:j + 1], pltpu.roll(v, nx - 1, 1))

        def side_z(v, s, c, y):
            return jnp.where(row == nz - 1, rz[s, c, y:y + 1, :], pltpu.roll(v, nz - 1, 0))

        for s in range(2):
            value = difference(e, s, y, lift, side_x, side_z)
            for c in range(3):
                h[s, c, y] = h[s, c, y] + -time_step * value[c]

    def front_x(n):
        hx, hy, hz = (rot_packed(v, x_ahead) for v in (unfold(xm_r[n, 1])[0], *unfold(xm_r[n, 0])))
        below = jnp.where(z_first, 0.0, rot_packed(unfold(xmzp_r[n])[0], x_ahead)[nz - 1:nz, :])
        hx_z = shift(hx, below, 0)
        side = rot_packed(rot_packed(unfold(xmyp_r[n])[0], x_ahead), y_behind)
        side = pltpu.roll(side, nx - (ny - 1), 1)
        first = jnp.logical_or(lane == 0, lane == ny)
        hx_y = jnp.where(first, side, pltpu.roll(hx, 1, 1))
        scale = time_step * kx[...]
        px[0] = px[0] - scale * ((hx - hx_z) - (hz - xp[n, 1]))
        px[1] = px[1] - scale * ((hy - xp[n, 0]) - (hx - hx_y))

    def front_z(n):
        scale = time_step * kz[...]
        side = rot(zmyp_r[n, 2:3, :], zmyp_r[n, 3:4, :], y_behind)
        corner = rot_packed(unfold(zmxp_r[n])[1], x_behind)[0:1, :]
        for s in range(2):
            hx, hy, hz = (zm_r[n, s, c] for c in range(3))
            hz_y = shift(hz, side[s], 0)
            column = jnp.sum(jnp.where(lane8 == s * ny + row8, corner, 0.0), axis=1, keepdims=True)
            hz_x = shift(hz, column, 1)
            e_x = rz[s, 0] - scale * ((hz - hz_y) - (hy - zp[n, s, 1]))
            e_y = rz[s, 1] - scale * ((hx - zp[n, s, 0]) - (hz - hz_x))
            rz[s, 0] = jnp.where(z_last, 0.0, e_x)
            rz[s, 1] = jnp.where(z_last, 0.0, e_y)

    def front_y(n):
        scale = time_step * ky[...]
        part_x = rot(ym_r[n, 0, 0], ym_r[n, 0, 1], y_ahead)
        part_z = rot(ym_r[n, 1, 0], ym_r[n, 1, 1], y_ahead)
        below = rot(ymzp_r[n, 0:1, :], ymzp_r[n, 1:2, :], y_ahead)
        corner = rot_packed(rot_packed(unfold(ymxp_r[n])[0], y_ahead), x_behind)
        for s in range(2):
            hy_z = jnp.where(row == 0, jnp.where(z_first, 0.0, below[s]), 0.0)
            hy_x = jnp.where(lane == 0, corner[:, s * ny:s * ny + 1], 0.0)
            ry[0, s] = part_x[s] + scale * (h[s, 2, ny - 1] - hy_z)
            ry[1, s] = part_z[s] + scale * (hy_x - h[s, 0, ny - 1])

    def send_part(n):
        scale = time_step * inv[0]
        for s in range(2):
            hx, hy, hz = (h[s, c, 0] for c in range(3))
            ys[n, 0, s] = e[s, 0, 0] - scale * (hz - (hy - shift(hy, 0.0, 0)))
            ys[n, 1, s] = e[s, 2, 0] - scale * ((hy - shift(hy, 0.0, 1)) - hx)

    def gradient(n):
        for y in range(ny):
            total = None
            for s in range(2):
                for c in range(3):
                    term = e[s, c, y] * fwd[n, s, c, y].astype(jnp.float32)
                    total = term if total is None else total + term
            total = inv[y] * total
            g[y] = total if n == 0 else g[y] + total

    now = copies(0)
    start(now, "yp0", "yp2", "em")
    load_h.wait()
    packed = [blank] * 5
    for y in range(ny):
        packed = pack(packed, 0, y)
    store_packed(packed, 0)
    start(now, "xp", "zp", "xm", "zm")
    start(now, *(name for name, _ in EDGES))
    load_mat.wait()
    load_eps.wait()
    table = [1.0 / jnp.full((nz, nx), eps[m], jnp.float32) for m in range(eps.shape[0])]

    def inverse(kind):
        value = table[0]
        for m in range(1, eps.shape[0]):
            value = jnp.where(kind == m, table[m], value)
        return value

    for y in range(ny):
        inv[y] = inverse(mat[y])
    load_e.wait()
    send_part(0)
    now["ym"].start()
    packed = [blank] * 3
    for y in range(ny):
        for s in range(2):
            for c in (1, 2):
                packed[c - 1] = put(packed[c - 1], e[s, c, y][:, 0:1], y, s)
            packed[2] = put(packed[2], inv[y][:, 0:1], y, s)
            for c in (0, 1):
                ez[2 * s + c, y:y + 1] = e[s, c, y, 0:1, :]
        ez[4, y:y + 1] = inv[y, 0:1, :]
    ex[0] = fold(packed[0], packed[1])
    ex[1] = fold(packed[2], None)
    start(now, "ex", "ez")

    for n in range(steps):
        landed(now, "xp", "zp")
        xb = [rot_packed(v, x_behind) for v in unfold(xp_r[n])]
        for y in range(1, ny):
            update_e(n, y, xb, None)
        landed(now, "yp0", "yp2")
        update_e(n, 0, xb, [rot(yp_r[n, i, 0], yp_r[n, i, 1], y_behind) for i in range(2)])
        if n == steps - 1:
            if n == 0:
                load_fwd.wait()
            gradient(n)
        if n == 0:
            landed(now, "ex", "ez", "em")
            ex_u = unfold(ex_r[0])
            for i in range(2):
                px[i] = rot_packed(ex_u[i], x_ahead)
                for c in range(2):
                    rz[i, c] = ez_r[2 * i + c]
            kx[...] = unfold(ex_r[1])[0]
            kz[...] = ez_r[4]
            ky[...] = inverse(em_r[...])
        landed(now, "xm", "zm", *(name for name, _ in EDGES))
        front_x(n)
        front_z(n)
        landed(now, "ym")
        front_y(n)
        for copy in now.values():
            copy.wait_send()
        if n == steps - 1:
            break
        packed = [blank] * 5
        later = copies(n + 1)
        for y in (0, ny - 1, *range(1, ny - 1)):
            update_h(y)
            packed = pack(packed, n + 1, y)
            if y == 0:
                send_part(n + 1)
                later["ym"].start()
            if y == ny - 1:
                start(later, "yp0", "yp2")
        store_packed(packed, n + 1)
        start(later, "xp", "zp", "xm", "zm")
        start(later, *(name for name, _ in EDGES))
        now = later
        if n == 0:
            load_fwd.wait()
        gradient(n)


def shards(counts, adj_e, adj_h, fwd_e, material, eps_table):
    ny, nz, nx = material.shape
    steps = fwd_e.shape[0]
    hbm = pl.BlockSpec(memory_space=pltpu.HBM)
    vmem = pl.BlockSpec(memory_space=pltpu.VMEM)
    f32 = jnp.float32
    e, h, g, px, ry, rz = pl.pallas_call(
        functools.partial(kernel, counts),
        out_shape=(
            pltpu.VMEM(adj_e.shape, f32),
            pltpu.VMEM(adj_h.shape, f32),
            pltpu.VMEM(material.shape, f32),
            pltpu.VMEM((2, nz, nx), f32),
            pltpu.VMEM((2, 2, nz, nx), f32),
            pltpu.VMEM((2, 2, ny, nx), f32),
        ),
        in_specs=[hbm] * 5,
        out_specs=[vmem] * 6,
        scratch_shapes=[
            pltpu.SMEM(eps_table.shape, f32),
            pltpu.VMEM(fwd_e.shape, fwd_e.dtype),
            pltpu.VMEM(material.shape, material.dtype),
            pltpu.VMEM(material.shape, f32),
            pltpu.VMEM((nz, nx), f32),
            pltpu.VMEM((nz, nx), f32),
            pltpu.VMEM((ny, nx), f32),
            *(pltpu.VMEM((steps, *shape), f32) for shape in (
                (2, nz, nx), (8, nx), (2, 8, nx), (8, nx), (2, 2, ny, nx), (2, 3, ny, nx),
                (8, nx), (2, 8, nx), (2, 2, nz, nx), (2, 2, nz, nx),
                (2, 2, ny, nx), (2, 3, ny, nx), *[(8, nx)] * 6)),
            pltpu.VMEM((2, 8, nx), f32),
            pltpu.VMEM((5, ny, nx), f32),
            pltpu.VMEM((2, 8, nx), f32),
            pltpu.VMEM((steps, 2, 2, nz, nx), f32),
            pltpu.VMEM((nz, nx), material.dtype),
            pltpu.VMEM((5, ny, nx), f32),
            pltpu.SemaphoreType.DMA((5,)),
            pltpu.SemaphoreType.DMA((steps, len(SENDS))),
            pltpu.SemaphoreType.DMA((steps, len(SENDS))),
        ],
        compiler_params=pltpu.CompilerParams(
            collective_id=0, has_side_effects=True, vmem_limit_bytes=24 * 1024 * 1024
        ),
    )(*(pltpu.with_memory_space_constraint(a, pltpu.HBM) for a in (eps_table, adj_e, adj_h, fwd_e, material)))
    return pl.pallas_call(
        finish,
        out_shape=(
            jax.ShapeDtypeStruct(adj_e.shape, f32),
            jax.ShapeDtypeStruct(adj_h.shape, f32),
            jax.ShapeDtypeStruct(material.shape, f32),
        ),
        in_specs=[vmem] * 6,
        out_specs=[hbm] * 3,
        scratch_shapes=[pltpu.VMEM(adj_h.shape, f32), pltpu.SemaphoreType.DMA((4,))],
        compiler_params=pltpu.CompilerParams(vmem_limit_bytes=8 * 1024 * 1024),
    )(e, g, h, px, ry, rz)


def solution(mesh):
    counts = {a: mesh.shape[a] for a in ("gx", "gy", "gz")}
    return jax.shard_map(
        functools.partial(shards, counts),
        mesh=mesh,
        in_specs=(
            P(None, None, "gy", "gz", "gx"),
            P(None, None, "gy", "gz", "gx"),
            P(None, None, None, "gy", "gz", "gx"),
            P("gy", "gz", "gx"),
            P(),
        ),
        out_specs=(
            P(None, None, "gy", "gz", "gx"),
            P(None, None, "gy", "gz", "gx"),
            P("gy", "gz", "gx"),
        ),
        check_vma=False,
    )
```
